32 devices in a mesh: dp: 2 (over x), wide: 16 (over z, y, core).
Axes of the slice: x: 2, y: 2, z: 4, core: 2. Of those that a mesh axis runs over, the one named last changes fastest.
Arguments:
- tokens: bfloat16 [4, 1024, 2048], P('dp', 'wide'), may hold values from -6 to 6
- lengths: int32 [4], P('dp'), may hold values from 128 to 1024, as said below
- gain_one: bfloat16 [2048], P('wide'), may hold values from 0.5 to 1.5
- shift_one: bfloat16 [2048], P('wide'), may hold values from -1 to 1
- w_qkv: bfloat16 [2048, 6144], P('wide'), may hold values from -0.125 to 0.125
- b_qkv: bfloat16 [6144], P('wide'), may hold values from -1 to 1
- w_dense: bfloat16 [2048, 2048], P('wide'), may hold values from -0.5 to 0.5
- b_dense: bfloat16 [2048], P('wide'), may hold values from -1 to 1
- gain_two: bfloat16 [2048], P('wide'), may hold values from 0.5 to 1.5
- shift_two: bfloat16 [2048], P('wide'), may hold values from -1 to 1
- w_up: bfloat16 [2048, 8192], P('wide'), may hold values from -0.125 to 0.125
- b_up: bfloat16 [8192], P('wide'), may hold values from -1 to 1
- w_down: bfloat16 [8192, 2048], P('wide'), may hold values from -0.0625 to 0.0625
- b_down: bfloat16 [2048], P('wide'), may hold values from -1 to 1
- cotangent: bfloat16 [4, 1024, 2048], P('dp', 'wide'), may hold values from -6 to 6
Outputs:
- mixed: bfloat16 [4, 1024, 2048], P('dp', 'wide')
- token_grad: bfloat16 [4, 1024, 2048], P('dp', 'wide')
- grad_gain_one: float32 [2048], P('wide')
- grad_shift_one: float32 [2048], P('wide')
- grad_w_qkv: float32 [2048, 6144], P('wide')
- grad_b_qkv: float32 [6144], P('wide')
- grad_w_dense: float32 [2048, 2048], P('wide')
- grad_b_dense: float32 [2048], P('wide')
- grad_gain_two: float32 [2048], P('wide')
- grad_shift_two: float32 [2048], P('wide')
- grad_w_up: float32 [2048, 8192], P('wide')
- grad_b_up: float32 [8192], P('wide')
- grad_w_down: float32 [8192, 2048], P('wide')
- grad_b_down: float32 [2048], P('wide')
The draws below stay inside these ranges and needn't reach their ends.
Inputs may be any that keep to these rules, and one draw needn't show every extreme that they name: `lengths`: in each group of 2 sequences [i * 2, (i + 1) * 2) one has length exactly 1024; exactly one sequence of all has length 128.
All inputs are finite; a program needn't handle non-finite values.
Results may differ from the reference program's by a relative error of at most 0.0092.
Values may be sent and summed in bfloat16 or wider, within the bound.
No kernel may reach another device: no remote copies, remote signals or barrier semaphores. Data moves between devices by JAX's collectives and lax.ppermute only.
A program may use at most 640 MiB of HBM per device.

```python
import jax
import jax.numpy as jnp
from jax import lax

D = 2048
HEADS = 8
HEAD_DIM = 256
FF = 8192
ROT = 64
SEQS = 2
MIN_LEN = 128
SEQ_LEN = 1024
NSEQ = 4


def draw_lengths(key, part):
    key = jax.random.fold_in(key, 11)
    key_base, key_long, key_offset, key_group = jax.random.split(key, 4)
    groups = NSEQ // SEQS
    picked = jax.random.randint(key_base, (groups, SEQS), MIN_LEN + 1, SEQ_LEN + 1)
    longest = jax.random.randint(key_long, (groups, 1), 0, SEQS)
    offset = jax.random.randint(key_offset, (groups, 1), 1, SEQS)
    shortest = (longest + offset) % SEQS
    short_group = jax.random.randint(key_group, (), 0, groups)
    column_ids = jnp.arange(SEQS)[None, :]
    group_ids = jnp.arange(groups)[:, None]
    picked = jnp.where(column_ids == longest, SEQ_LEN, picked)
    picked = jnp.where((column_ids == shortest) & (group_ids == short_group), MIN_LEN, picked)
    return picked.reshape(NSEQ).astype(jnp.int32)


def shard_levels(stream_key, dims, pieces, least, top_value):
    level, own = 1.0, jax.random.fold_in(stream_key, 6)
    for dim, parts in pieces:
        draws = jnp.exp(jax.random.uniform(jax.random.fold_in(own, dim), (parts,), jnp.float32, least / len(pieces), top_value / len(pieces)))
        level = level * jnp.repeat(draws, dims[dim] // parts).reshape([-1 if axis == dim else 1 for axis in range(len(dims))])
    return level


def normal_values(own_key, extent, width, limit, shards=(), kind=jnp.bfloat16):
    drawn = width * jax.random.normal(own_key, extent, jnp.float32)
    if shards:
        drawn = drawn * shard_levels(own_key, extent, shards, -0.22, 0.18)
    return jnp.clip(drawn, -limit, limit).astype(kind)


def setup_inputs(seed: int = 0) -> dict:
    keys = jax.random.split(jax.random.key(seed), 16)
    tokens = normal_values(keys[0], (NSEQ, SEQ_LEN, D), 1.0, 6.0, ((0, 2), (1, 16)))
    lengths = draw_lengths(jax.random.fold_in(keys[15], 71), 0)
    gain_one = jnp.clip(1.0 + 0.1 * jax.random.normal(keys[2], (D,), jnp.float32), 0.5, 1.5).astype(jnp.bfloat16)
    shift_one = normal_values(keys[3], (D,), 0.2, 1.0, ((0, 16),))
    w_qkv = normal_values(keys[4], (D, 3 * D), D ** -0.5, 0.125, ((0, 16),))
    b_qkv = normal_values(keys[5], (3 * D,), 0.2, 1.0, ((0, 16),))
    w_dense = normal_values(keys[6], (D, D), (D // 16) ** -0.5, 0.5, ((0, 16),))
    b_dense = normal_values(keys[7], (D,), 0.2, 1.0, ((0, 16),))
    gain_two = jnp.clip(1.0 + 0.1 * jax.random.normal(keys[8], (D,), jnp.float32), 0.5, 1.5).astype(jnp.bfloat16)
    shift_two = normal_values(keys[9], (D,), 0.2, 1.0, ((0, 16),))
    w_up = normal_values(keys[10], (D, FF), D ** -0.5, 0.125, ((0, 16),))
    b_up = normal_values(keys[11], (FF,), 0.2, 1.0, ((0, 16),))
    w_down = normal_values(keys[12], (FF, D), FF ** -0.5, 0.0625, ((0, 16),))
    b_down = normal_values(keys[13], (D,), 0.2, 1.0, ((0, 16),))
    cotangent = normal_values(keys[14], (NSEQ, SEQ_LEN, D), 1.0, 6.0, ((0, 2), (1, 16)))
    return dict(tokens=tokens, lengths=lengths, gain_one=gain_one, shift_one=shift_one, w_qkv=w_qkv, b_qkv=b_qkv, w_dense=w_dense, b_dense=b_dense, gain_two=gain_two, shift_two=shift_two, w_up=w_up, b_up=b_up, w_down=w_down, b_down=b_down, cotangent=cotangent)


EPS = 1e-05
MASKED = -1e+30
ROT_BASE = 10000.0
ROOT_HALF = 0.7071067811865476
HIGHEST = lax.Precision.HIGHEST

@jax.custom_vjp
def low(v):
    return lax.optimization_barrier(v.astype(jnp.bfloat16)).astype(jnp.float32)

@jax.custom_vjp
def low_back(v):
    return v

def low_keep(v):
    return (low(v), None)

def low_pass(kept, grad):
    return (grad,)

def back_keep(v):
    return (v, None)

def back_low(kept, grad):
    return (low(grad),)
low.defvjp(low_keep, low_pass)
low_back.defvjp(back_keep, back_low)

def gelu_exact(values):
    return 0.5 * values * (1.0 + jax.scipy.special.erf(values * ROOT_HALF))

def norm_core(values, gain_vec):
    average = lax.optimization_barrier(jnp.mean(values, axis=-1, keepdims=True))
    centered = values - average
    variance = lax.optimization_barrier(jnp.mean(centered * centered, axis=-1, keepdims=True))
    return centered * lax.rsqrt(variance + EPS) * gain_vec

def rotary_tables(places):
    halves = ROT // 2
    inverse = ROT_BASE ** (-2.0 * jnp.arange(halves, dtype=jnp.float32) / ROT)
    angles = places.astype(jnp.float32)[:, None] * inverse[None, :]
    return (jnp.cos(angles), jnp.sin(angles))

def rotate(head_rows, cosine, sine_table):
    halves = ROT // 2
    first = head_rows[..., :halves]
    second = head_rows[..., halves:ROT]
    cosine_col = cosine[:, None, :]
    sine_col = sine_table[:, None, :]
    return jnp.concatenate([first * cosine_col - second * sine_col, second * cosine_col + first * sine_col, head_rows[..., ROT:]], axis=-1)

def attention_core(queries, key_rows, value_rows, length):
    places = jnp.arange(SEQ_LEN)
    allowed = (places[None, :] <= places[:, None]) & (places[None, :] < length)
    scores = jnp.einsum('qhd,khd->hqk', queries, key_rows, precision=HIGHEST) * HEAD_DIM ** (-0.5)
    scores = low_back(scores)
    masked = jnp.where(allowed[None], scores, MASKED)
    highest = lax.optimization_barrier(jnp.max(masked, axis=-1, keepdims=True))
    raised = jnp.exp(masked - highest)
    soft_probs = low(raised / lax.optimization_barrier(jnp.sum(raised, axis=-1, keepdims=True)))
    return jnp.einsum('hqk,khd->qhd', soft_probs, value_rows, precision=HIGHEST)

def sequence_layer(row_tokens, length, params):
    gain_one, shift_one, w_qkv, b_qkv, w_dense, b_dense, gain_two, shift_two, w_up, b_up, w_down, b_down = params
    places = jnp.arange(SEQ_LEN)
    normed_one = low(norm_core(row_tokens, gain_one) + shift_one)
    joined_qkv = low_back(jnp.dot(normed_one, w_qkv, precision=HIGHEST) + b_qkv)
    cosine, sine_table = rotary_tables(places)
    queries = low(rotate(joined_qkv[:, :D].reshape(SEQ_LEN, HEADS, HEAD_DIM), cosine, sine_table))
    key_rows = low(rotate(joined_qkv[:, D:2 * D].reshape(SEQ_LEN, HEADS, HEAD_DIM), cosine, sine_table))
    value_rows = low(joined_qkv[:, 2 * D:].reshape(SEQ_LEN, HEADS, HEAD_DIM))
    attended = attention_core(queries, key_rows, value_rows, length)
    attended = low(low_back(attended.reshape(SEQ_LEN, D)))
    branch_attn = jnp.dot(attended, w_dense, precision=HIGHEST) + b_dense
    normed_two = low(norm_core(row_tokens, gain_two) + shift_two)
    upper_in = low_back(jnp.dot(normed_two, w_up, precision=HIGHEST) + b_up)
    activated = low(gelu_exact(upper_in))
    branch_mlp = jnp.dot(activated, w_down, precision=HIGHEST) + b_down
    valid_rows = (places < length).astype(jnp.float32)[:, None]
    return valid_rows * (row_tokens + branch_attn + branch_mlp)

def reference(tokens, lengths, gain_one, shift_one, w_qkv, b_qkv, w_dense, b_dense, gain_two, shift_two, w_up, b_up, w_down, b_down, cotangent):
    params = tuple((weight.astype(jnp.float32) for weight in (gain_one, shift_one, w_qkv, b_qkv, w_dense, b_dense, gain_two, shift_two, w_up, b_up, w_down, b_down)))

    def forward(inputs, weights_all):

        def per_sequence(packed):
            return sequence_layer(packed[0], packed[1], weights_all)
        return lax.map(jax.checkpoint(per_sequence), (inputs, lengths))
    result, pullback = jax.vjp(forward, tokens.astype(jnp.float32), params)
    token_grad, grads = pullback(cotangent.astype(jnp.float32))
    return (result.astype(jnp.bfloat16), token_grad.astype(jnp.bfloat16), grads[0], grads[1], grads[2], grads[3], grads[4], grads[5], grads[6], grads[7], grads[8], grads[9], grads[10], grads[11])
```

```python
import jax
import jax.numpy as jnp
from jax import lax
from jax.sharding import Mesh
from jax.sharding import PartitionSpec as P

HEADS = 8
HEAD_DIM = 256
ROT = 64

EPS = 1e-05
MASKED = -1e30
ROT_BASE = 10000.0
ROOT_HALF = 0.7071067811865476
INV_ROOT_TAU = 0.3989422804014327

WIDE = ("head", "sub")
f32 = jnp.float32
bf16 = jnp.bfloat16


def rotary_tables(places):
    halves = ROT // 2
    inverse = ROT_BASE ** (-2.0 * jnp.arange(halves, dtype=f32) / ROT)
    angles = places.astype(f32)[:, None] * inverse[None, :]
    return (jnp.cos(angles), jnp.sin(angles))


def rotate(rows, cosine, sine):
    halves = ROT // 2
    first = rows[..., :halves]
    second = rows[..., halves:ROT]
    return jnp.concatenate(
        [
            first * cosine - second * sine,
            second * cosine + first * sine,
            rows[..., ROT:],
        ],
        axis=-1,
    )


def norm_stats(values):
    average = jnp.mean(values, axis=-1, keepdims=True)
    centered = values - average
    variance = jnp.mean(centered * centered, axis=-1, keepdims=True)
    scale = lax.rsqrt(variance + EPS)
    return (centered * scale, scale)


def exchange(parts, count):
    me = lax.axis_index("sub")
    got = []
    for shift in range(count):
        part = parts(lax.rem(me + shift, count))
        if shift:
            part = lax.ppermute(part, "sub", [(j, (j + shift) % count) for j in range(count)])
        got.append(part)
    stacked = jnp.stack(got)
    order = lax.rem(me - jnp.arange(count, dtype=jnp.int32) + count, count)
    if count == 2:
        return jnp.where(me == 0, stacked, stacked[::-1])
    return jnp.take(stacked, order, axis=0)


def over_dp(low):
    count = lax.axis_size("dp")
    if count == 2:
        other = lax.ppermute(low, "dp", [(0, 1), (1, 0)])
        return low.astype(f32) + other.astype(f32)
    return lax.psum(low.astype(f32), "dp")


def dot(a, b, dims, out=f32):
    return lax.dot_general(a, b, (dims, ((), ())), preferred_element_type=f32).astype(out)


NN = ((1,), (0,))
NT = ((1,), (1,))
TN = ((0,), (0,))


def local(
    tokens,
    lengths,
    gain_one,
    shift_one,
    w_qkv,
    b_qkv,
    w_dense,
    b_dense,
    gain_two,
    shift_two,
    w_up,
    b_up,
    w_down,
    b_down,
    cotangent,
):
    S, span, D = tokens.shape
    M = lax.axis_size("sub")
    W = lax.axis_size("head") * M
    G = M // S
    L = span * W
    T = S * L
    R = w_qkv.shape[0]
    CW = D // W
    FW = w_down.shape[0]
    FF = w_up.shape[1]
    me = lax.axis_index(WIDE)
    sub = lax.axis_index("sub")
    own_seq = sub // G
    own_chunk = lax.rem(sub, G)
    Q = L // G

    small = jnp.concatenate([gain_one, shift_one, gain_two, shift_two, b_qkv, b_dense, b_down])
    small_all = lax.all_gather(small, WIDE)
    pieces = []
    start = 0
    for piece in (gain_one, shift_one, gain_two, shift_two, b_qkv, b_dense, b_down):
        pieces.append(small_all[:, start : start + piece.shape[0]].reshape(-1).astype(f32))
        start += piece.shape[0]
    g1, s1, g2, s2, bq_all, bd_all, bo_all = pieces
    bq = lax.dynamic_index_in_dim(bq_all.reshape(3, W, CW), me, 1, keepdims=False).reshape(3 * CW)

    x_all = lax.all_gather(tokens, WIDE)
    c_all = lax.all_gather(cotangent, WIDE)

    sent = jnp.concatenate(
        [
            w_qkv.reshape(R, 3, W, CW).transpose(2, 0, 1, 3).reshape(W, R, 3 * CW),
            w_up.reshape(R, W, FW).transpose(1, 0, 2),
        ],
        axis=-1,
    )
    cols = lax.all_to_all(sent, WIDE, 0, 0, tiled=True).reshape(D, 3 * CW + FW)
    wq, wu = cols[:, : 3 * CW], cols[:, 3 * CW :]
    wo = jnp.concatenate([w_down, w_dense], axis=0)

    place = (
        jnp.arange(W, dtype=jnp.int32)[:, None, None] * span
        + jnp.arange(span, dtype=jnp.int32)[None, None, :]
    )
    valid = (place < lengths[None, :, None]).reshape(T, 1)
    go = jnp.where(valid, c_all.reshape(T, D), jnp.zeros((), bf16))

    n_all, _ = norm_stats(x_all.reshape(T, D).astype(f32))
    h1 = (n_all * g1 + s1).astype(bf16)
    h2 = (n_all * g2 + s2).astype(bf16)

    joined = dot(h1, wq, NN) + bq
    cosine, sine = rotary_tables(jnp.arange(L, dtype=jnp.int32))
    early = CW >= ROT
    joined = joined.reshape(W, S, span, 3, CW)
    if early:
        here = sub == 0 if HEAD_DIM // CW > 1 else True
        cos_w = jnp.where(here, cosine, 1.0).reshape(W, 1, span, 1, ROT // 2)
        sin_w = jnp.where(here, sine, 0.0).reshape(W, 1, span, 1, ROT // 2)
        joined = jnp.concatenate(
            [rotate(joined[..., :2, :], cos_w, sin_w), joined[..., 2:, :]], axis=3
        ).astype(bf16)

    def columns_of(i):
        return lax.dynamic_index_in_dim(joined, i // G, 1, keepdims=False).reshape(L, 3, CW)

    heads = exchange(columns_of, M).transpose(2, 1, 0, 3).reshape(3, L, M * CW)
    if not early:
        heads = jnp.stack(
            [rotate(heads[0], cosine, sine), rotate(heads[1], cosine, sine), heads[2]]
        ).astype(bf16)
    queries = lax.dynamic_slice_in_dim(heads[0], own_chunk * Q, Q, 0)
    keys, values = heads[1], heads[2]

    length = lax.dynamic_index_in_dim(lengths, own_seq, 0, keepdims=False)
    q_places = own_chunk * Q + jnp.arange(Q, dtype=jnp.int32)
    k_places = jnp.arange(L, dtype=jnp.int32)
    allowed = (k_places[None, :] <= q_places[:, None]) & (k_places[None, :] < length)
    score_scale = HEAD_DIM ** (-0.5)
    scores = jnp.where(allowed, dot(queries, keys, NT) * score_scale, MASKED)
    raised = jnp.exp(scores - jnp.max(scores, axis=-1, keepdims=True))
    soft = raised / jnp.sum(raised, axis=-1, keepdims=True)
    soft_low = soft.astype(bf16)
    attended = dot(soft_low, values, NN, bf16)

    def attended_of(i):
        return lax.dynamic_slice_in_dim(attended, i * CW, CW, 1)

    att = exchange(attended_of, M).reshape(S, W, span, CW).transpose(1, 0, 2, 3).reshape(T, CW)

    upper = dot(h2, wu, NN) + b_up.astype(f32)
    cdf = 0.5 * (1.0 + lax.erf(upper * ROOT_HALF))
    act = (upper * cdf).astype(bf16)
    slope = cdf + upper * jnp.exp(-0.5 * upper * upper) * INV_ROOT_TAU

    both = jnp.concatenate([act, att], axis=1)
    mixed_part = dot(both, wo, NN, bf16).reshape(W, S * span, D)
    mixed_own = lax.psum_scatter(mixed_part, WIDE, scatter_dimension=0, tiled=True).reshape(
        S, span, D
    )
    own_place = me * span + jnp.arange(span, dtype=jnp.int32)
    own_valid = (own_place[None, :] < lengths[:, None])[:, :, None]
    x_own = tokens.astype(f32)
    mixed = jnp.where(own_valid, x_own + mixed_own.astype(f32) + (bd_all + bo_all), 0.0).astype(bf16)

    grad_both = dot(go, wo, NT)
    gu = (grad_both[:, :FW] * slope).astype(bf16)
    ga = grad_both[:, FW:].astype(bf16).reshape(W, S, span, CW)

    def grads_of(i):
        part = lax.dynamic_index_in_dim(ga, i // G, 1, keepdims=False).reshape(L, CW)
        return lax.dynamic_slice_in_dim(part, lax.rem(i, G) * Q, Q, 0)

    g_att = exchange(grads_of, M).transpose(1, 0, 2).reshape(Q, M * CW)
    g_soft = dot(g_att, values, NT)
    delta = jnp.sum(soft * g_soft, axis=-1, keepdims=True)
    g_scores = (soft * (g_soft - delta)).astype(bf16)
    g_q = dot(g_scores, keys, NN) * score_scale
    g_k = dot(g_scores, queries, TN) * score_scale
    g_v = dot(soft_low, g_att, TN)
    if G > 1:
        g_q = lax.dynamic_update_slice_in_dim(
            jnp.zeros((L, M * CW), f32), g_q, own_chunk * Q, 0
        )
    g_joined = jnp.stack(
        [rotate(g_q, cosine, -sine), rotate(g_k, cosine, -sine), g_v], axis=1
    ).astype(bf16)

    def joined_of(i):
        return lax.dynamic_slice_in_dim(g_joined, i * CW, CW, 2)

    gj = exchange(joined_of, M).reshape(S, G, L, 3, CW)
    gj = gj[:, 0] if G == 1 else jnp.sum(gj.astype(f32), axis=1).astype(bf16)
    gj = gj.reshape(S, W, span, 3 * CW).transpose(1, 0, 2, 3).reshape(T, 3 * CW)

    back = jnp.concatenate([gj, gu], axis=1)
    w_back = jnp.concatenate(
        [(wq.astype(f32) * g1[:, None]).astype(bf16), (wu.astype(f32) * g2[:, None]).astype(bf16)],
        axis=1,
    )
    f_part = dot(back, w_back, NT, bf16).reshape(W, S * span, D)
    f_own = (
        lax.psum_scatter(f_part, WIDE, scatter_dimension=0, tiled=True)
        .reshape(S, span, D)
        .astype(f32)
    )
    n_own, r_own = norm_stats(x_own)
    grad_x = r_own * (
        f_own
        - jnp.mean(f_own, axis=-1, keepdims=True)
        - n_own * jnp.mean(f_own * n_own, axis=-1, keepdims=True)
    )
    go_own = jnp.where(own_valid, cotangent.astype(f32), 0.0)
    token_grad = (go_own + grad_x).astype(bf16)

    gw_out = dot(both, go, TN, bf16)
    gw_out = over_dp(gw_out)
    go_cols = lax.dynamic_slice_in_dim(go, me * CW, CW, 1)
    gb_out = jnp.sum(go_cols.astype(f32), axis=0)
    gb_up = jnp.sum(gu.astype(f32), axis=0)
    gb_q = jnp.sum(gj.astype(f32), axis=0)
    tail = 8

    def to_rows(grad, bias):
        width = grad.shape[1]
        block = jnp.concatenate(
            [
                grad.reshape(W, R, width),
                jnp.broadcast_to(bias.astype(bf16)[None, None, :], (W, tail, width)),
            ],
            axis=1,
        )
        got = over_dp(lax.all_to_all(block, WIDE, 0, 0, tiled=True))
        return (got[:, :R].transpose(1, 0, 2), got[:, R])

    gw_up, gb_up_all = to_rows(dot(h2, gu, TN, bf16), gb_up)
    gw_q, gb_q_all = to_rows(dot(h1, gj, TN, bf16), gb_q)
    gw_up = gw_up.reshape(R, FF)
    gw_q = gw_q.reshape(R, W, 3, CW).transpose(0, 2, 1, 3).reshape(R, 3 * D)
    gb_up_all = gb_up_all.reshape(FF)
    gb_q_all = gb_q_all.reshape(W, 3, CW).transpose(1, 0, 2).reshape(3 * D)

    def norm_grads(gw, gb, w, gain, shift):
        wf = w.astype(f32)
        shift_grad = jnp.sum(wf * gb[None, :], axis=1)
        gain_grad = (jnp.sum(wf * gw, axis=1) - shift.astype(f32) * shift_grad) / gain.astype(f32)
        return (gain_grad, shift_grad)

    gg1, gs1 = norm_grads(gw_q, gb_q_all, w_qkv, gain_one, shift_one)
    gg2, gs2 = norm_grads(gw_up, gb_up_all, w_up, gain_two, shift_two)
    gb_q_own = lax.dynamic_slice_in_dim(gb_q_all, me * 3 * CW, 3 * CW, 0)
    vectors = over_dp(jnp.concatenate([gb_out, gb_up]).astype(bf16))
    gb_out, gb_up = vectors[:CW], vectors[CW:]
    return (
        mixed,
        token_grad,
        gg1,
        gs1,
        gw_q,
        gb_q_own,
        gw_out[FW:],
        gb_out,
        gg2,
        gs2,
        gw_up,
        gb_up,
        gw_out[:FW],
        gb_out,
    )


def solution(mesh):
    dp, wide = mesh.shape["dp"], mesh.shape["wide"]
    split = Mesh(mesh.devices.reshape(dp, HEADS, wide // HEADS), ("dp",) + WIDE)
    rows = P("dp", WIDE, None)
    mat, vec = P(WIDE, None), P(WIDE)
    in_specs = (rows, P("dp"), vec, vec, mat, vec, mat, vec, vec, vec, mat, vec, mat, vec, rows)
    out_specs = (rows, rows, vec, vec, mat, vec, mat, vec, vec, vec, mat, vec, mat, vec)
    return jax.shard_map(local, mesh=split, in_specs=in_specs, out_specs=out_specs, check_vma=False)
```

```python
import functools
import math

import jax
import jax.numpy as jnp
from jax import lax
from jax.experimental import pallas as pl
from jax.experimental.pallas import tpu as pltpu
from jax.sharding import Mesh
from jax.sharding import PartitionSpec as P

HEADS = 8
HEAD_DIM = 256
ROT = 64

EPS = 1e-05
MASKED = -1e30
ROT_BASE = 10000.0
ROOT_HALF = 0.7071067811865476
INV_ROOT_TAU = 0.3989422804014327

WIDE = ("z", "y", "core")
CHIPS = ("z", "y")
TAIL = 8
BLOCK = 256
VMEM_BYTES = 58 * 1024 * 1024
f32 = jnp.float32
bf16 = jnp.bfloat16


def rotary_tables(places):
    halves = ROT // 2
    inverse = ROT_BASE ** (-2.0 * jnp.arange(halves, dtype=f32) / ROT)
    angles = places.astype(f32)[:, None] * inverse[None, :]
    return (jnp.cos(angles), jnp.sin(angles))


def norm_stats(values):
    average = jnp.mean(values, axis=-1, keepdims=True)
    centered = values - average
    variance = jnp.mean(centered * centered, axis=-1, keepdims=True)
    scale = lax.rsqrt(variance + EPS)
    return (centered * scale, scale)


def swap(part, axis):
    return lax.ppermute(part, axis, [(0, 1), (1, 0)])


def pair(index, own, other, axis=0):
    return jnp.where(
        index == 0, jnp.stack([own, other], axis=axis), jnp.stack([other, own], axis=axis)
    )


def dot(a, b, dims, out=f32):
    return lax.dot_general(a, b, (dims, ((), ())), preferred_element_type=f32).astype(out)


NN = ((1,), (0,))
NT = ((1,), (1,))
TN = ((0,), (0,))


def pick(array, index, axis=0):
    return lax.dynamic_index_in_dim(array, index, axis, keepdims=False)


def gather_rows(own):
    return lax.all_gather(own, CHIPS, axis=0, tiled=True)


def rows_kernel(d, own, other, w, out, sums):
    @pl.when(pl.program_id(0) == 0)
    def _():
        sums[...] = jnp.zeros_like(sums)

    half = out.shape[0] // 2
    width = own.shape[2]
    for j in range(own.shape[0]):
        cols = slice(j * width, (j + 1) * width)
        mine, got = own[j].astype(f32), other[j].astype(f32)
        bias = mine[half : half + 1] + got[half : half + 1]
        for at in range(2):
            rows = slice(at * half, (at + 1) * half)
            grad = jnp.where(d[0] == at, mine[:half], got[:half])
            out[rows, cols] = grad
            weight = w[rows, cols].astype(f32)
            sums[rows, 0:1] += jnp.sum(weight * grad, axis=1, keepdims=True)
            sums[rows, 1:2] += jnp.sum(weight * bias, axis=1, keepdims=True)


def weight_rows(name, d, own, other, w, width, order=()):
    devices, height, columns = own.shape
    rows = w.shape[0]
    group = math.gcd(2048 // width, devices)
    blocks = devices // group
    shape = (group, height, width)
    at = lambda i: (lax.rem(i, blocks), 0, lax.div(i, blocks))
    grad, sums = call(
        rows_kernel,
        name,
        blocks * (columns // width),
        [
            (d, "scalars"),
            (own, shape, at),
            (other, shape, at),
            (w, (rows, group * width), lambda i: (0, i)),
        ],
        [((rows, w.shape[1]), f32, (rows, group * width), lambda i: (0, i)), ((rows, 2), f32, None)],
        order=order,
    )
    return (grad, sums[:, 0], sums[:, 1])


def half_kernel(mine, got, row, out):
    total = (mine[...].astype(f32) + got[...].astype(f32)).astype(bf16)
    tail = (out.shape[0], out.shape[1] - total.shape[1], out.shape[2])
    row = jnp.broadcast_to(row[...][None], tail).astype(bf16)
    out[...] = jnp.concatenate([total, row], axis=1)


def half_sum(name, mine, send, row, order):
    devices, rows, width = mine.shape
    return call(
        half_kernel,
        name,
        1,
        [(mine, None), (swap(send, "dp"), None), (row.reshape(1, width), None)],
        [((devices, rows + TAIL, width), bf16, None)],
        order=order,
    )[0]


def gate(value, *others):
    spec = pl.BlockSpec(memory_space=pl.ANY)
    return pl.pallas_call(
        lambda *refs: None,
        in_specs=[spec] * (1 + len(others)),
        out_specs=spec,
        out_shape=jax.ShapeDtypeStruct(value.shape, value.dtype),
        input_output_aliases={0: 0},
        name="gate",
    )(value, *others)


def scatter_rows(part):
    return lax.psum_scatter(part, CHIPS, scatter_dimension=0, tiled=True).astype(f32)


def call(kernel, name, grid, ins, outs, scratch=(), order=(), flops=0):
    def whole(shape):
        return pl.BlockSpec(shape, lambda i: (0,) * len(shape))

    def blocked(shape, block, at=None):
        if block == "scalars":
            return pl.BlockSpec(memory_space=pltpu.SMEM)
        if block is None:
            return whole(shape)
        return pl.BlockSpec(block, at or (lambda i: (i,) + (0,) * (len(block) - 1)))

    def run(*refs):
        kernel(*refs[: len(ins)], *refs[len(ins) + len(order) :])

    arrays = [entry[0] for entry in ins]
    moved = sum(a.size * a.dtype.itemsize for a in arrays)
    moved += sum(functools.reduce(lambda p, n: p * n, o[0], 1) * o[1].dtype.itemsize for o in outs)
    return pl.pallas_call(
        run,
        grid=(grid,),
        in_specs=[blocked(entry[0].shape, *entry[1:]) for entry in ins]
        + [pl.BlockSpec(memory_space=pl.ANY)] * len(order),
        out_specs=[blocked(o[0], *o[2:]) for o in outs],
        out_shape=[jax.ShapeDtypeStruct(o[0], o[1]) for o in outs],
        scratch_shapes=list(scratch),
        compiler_params=pltpu.CompilerParams(
            vmem_limit_bytes=VMEM_BYTES, dimension_semantics=("arbitrary",)
        ),
        cost_estimate=pl.CostEstimate(flops=flops, bytes_accessed=moved, transcendentals=0),
        name=name,
    )(*arrays, *order)


def turn(half, c_ref, down_ref, up_ref, way):
    width, step = half.shape[-1], ROT // 2
    ahead = pltpu.roll(half, width - step, 1) * down_ref
    behind = pltpu.roll(half, step, 1) * up_ref
    return half * c_ref + way * (behind - ahead)


def part_rows(at, total, own, other):
    rows = own.shape[0]
    first = at[0] == 0
    own[...] = jnp.where(first, total[:rows], total[rows:])
    other[...] = jnp.where(first, total[rows:], total[:rows])


def front_kernel(x, ok, norms, wuo, wux, wqo, wqx, bu, bq, cos, low, high, h1, h2, acto, actx, slo, slx, q, k, v):
    n, _ = norm_stats(x[...].astype(f32))
    first = (n * norms[0:1, :] + norms[1:2, :]).astype(bf16)
    second = (n * norms[2:3, :] + norms[3:4, :]).astype(bf16)
    h1[...] = first
    h2[...] = second
    for at, (w, act, slope) in enumerate(((wuo, acto, slo), (wux, actx, slx))):
        upper = dot(second, w[...], NN) + bu[at : at + 1, :]
        cdf = 0.5 * (1.0 + lax.erf(upper * ROOT_HALF))
        act[...] = (upper * cdf * ok[...]).astype(bf16)
        slope[...] = cdf + upper * jnp.exp(-0.5 * upper * upper) * INV_ROOT_TAU
    for at, w in enumerate((wqo, wqx)):
        joined = dot(first, w[...], NN) + bq[at : at + 1, :]
        wide = joined.shape[1] // 3
        cols = slice(at * wide, (at + 1) * wide)
        tables = (cos[:, cols], low[:, cols], high[:, cols])
        q[:, cols] = turn(joined[:, :wide], *tables, 1.0).astype(bf16)
        k[:, cols] = turn(joined[:, wide : 2 * wide], *tables, 1.0).astype(bf16)
        v[:, cols] = joined[:, 2 * wide :].astype(bf16)


def weights_of(q, k, row_place, col_place, scale):
    scores = dot(q, k, NT) * scale
    return jnp.where(col_place <= row_place, scores, MASKED)


def attend_kernel(scale, q, k, v, ok, row_place, col_place, att, lse):
    rows = q.shape[0]
    step = min(BLOCK, rows)
    for start in range(0, rows, step):
        mine, seen = slice(start, start + step), slice(0, start + step)
        scores = weights_of(q[mine, :], k[seen, :], row_place[mine, :], col_place[:, seen], scale)
        top = jnp.max(scores, axis=1, keepdims=True)
        raised = jnp.exp(scores - top)
        total = jnp.sum(raised, axis=1, keepdims=True)
        weights = (raised * (1.0 / total)).astype(bf16)
        att[mine, :] = (dot(weights, v[seen, :], NN) * ok[mine, :]).astype(bf16)
        lse[mine, :] = top + jnp.log(total)


def attend_back_kernel(scale, q, k, v, ga, lse, row_place, col_place, cos, low, high, gjo, gjx, sums, gk, gv):
    rows = q.shape[0]
    step = min(BLOCK, rows)
    gk[...] = jnp.zeros_like(gk)
    gv[...] = jnp.zeros_like(gv)
    wide = q.shape[1] // 2
    for start in range(0, rows, step):
        mine, seen = slice(start, start + step), slice(0, start + step)
        scores = weights_of(q[mine, :], k[seen, :], row_place[mine, :], col_place[:, seen], scale)
        soft = jnp.exp(scores - lse[mine, :])
        g_soft = dot(ga[mine, :], v[seen, :], NT)
        product = soft * g_soft
        delta = jnp.sum(product, axis=1, keepdims=True)
        g_scores = (product - soft * delta).astype(bf16)
        gk[seen, :] += dot(g_scores, q[mine, :], TN)
        gv[seen, :] += dot(soft.astype(bf16), ga[mine, :], TN)
        g_q = dot(g_scores, k[seen, :], NN) * scale
        for at, out in enumerate((gjo, gjx)):
            cols = slice(at * wide, (at + 1) * wide)
            tables = (cos[mine, cols], low[mine, cols], high[mine, cols])
            out[mine, :wide] = turn(g_q[:, cols], *tables, -1.0).astype(bf16)
    for start in range(0, rows, step):
        mine = slice(start, start + step)
        for at, out in enumerate((gjo, gjx)):
            cols = slice(at * wide, (at + 1) * wide)
            tables = (cos[mine, cols], low[mine, cols], high[mine, cols])
            out[mine, wide : 2 * wide] = turn(gk[mine, cols] * scale, *tables, -1.0).astype(bf16)
            out[mine, 2 * wide :] = gv[mine, cols].astype(bf16)
    for at, out in enumerate((gjo, gjx)):
        sums[at : at + 1, :] = jnp.sum(out[...].astype(f32), axis=0, keepdims=True)


def out_kernel(acto, actx, att, wo, wx, wd, out, done):
    total = dot(acto[...], wo[...], NN) + dot(actx[...], wx[...], NN) + dot(att[...], wd[...], NN)
    out[...] = total.astype(bf16)
    done[...] = jnp.zeros_like(done)


def back_kernel(c, ok, slo, slx, wo, wx, wd, guo, gux, ga, sums, sum_go):
    @pl.when(pl.program_id(0) == 0)
    def _():
        sums[...] = jnp.zeros_like(sums)
        sum_go[...] = jnp.zeros_like(sum_go)

    grad = jnp.where(ok[...] > 0, c[...], jnp.zeros((), bf16))
    for at, (w, slope, gu) in enumerate(((wo, slo, guo), (wx, slx, gux))):
        low = (dot(grad, w[...], NT) * slope[...]).astype(bf16)
        gu[...] = low
        sums[at : at + 1, :] += jnp.sum(low.astype(f32), axis=0, keepdims=True)
    ga[...] = dot(grad, wd[...], NT, bf16)
    sum_go[...] += jnp.sum(grad.astype(f32), axis=0, keepdims=True)


def in_kernel(gjo, gjx, guo, gux, wqo, wqx, wuo, wux, norms, out, done):
    one = dot(gjo[...], wqo[...], NT) + dot(gjx[...], wqx[...], NT)
    two = dot(guo[...], wuo[...], NT) + dot(gux[...], wux[...], NT)
    out[...] = (one * norms[0:1, :] + two * norms[2:3, :]).astype(bf16)
    done[...] = jnp.zeros_like(done)


def turned_kernel(left, right, *rest):
    total = dot(left[...], right[...], TN)
    if len(rest) == 2:
        total = total + rest[0][...].astype(f32)
    rest[-1][...] = total.astype(bf16)


def turned_half_kernel(d, left, right, got, mine, other):
    total = (dot(left[...], right[...], TN) + got[...].astype(f32)).astype(bf16)
    rows = mine.shape[1]
    for i in range(mine.shape[0]):
        at = slice(2 * i * rows, 2 * (i + 1) * rows)
        part_rows(d, total[at], mine.at[i], other.at[i])


def turned_product(name, left, right, got=None, start=0, count=None, halves=None, order=()):
    depth = left.shape[0]
    count = count or left.shape[1] - start
    width = right.shape[1]
    block = math.gcd(BLOCK, count)
    first = start // block
    ins = [(left, (depth, block), lambda i: (0, first + i)), (right, None)]
    if got is not None:
        ins.append((got, (block, width)))
    if halves:
        place, rows = halves
        blocks = (block // (2 * rows), rows, width)
        return call(
            turned_half_kernel,
            name,
            count // block,
            [(place, "scalars")] + ins,
            [((count // (2 * rows), rows, width), bf16, blocks)] * 2,
            order=order,
            flops=2 * depth * count * width,
        )
    return call(
        turned_kernel,
        name,
        count // block,
        ins,
        [((count, width), bf16, (block, width))],
        order=order,
        flops=2 * depth * count * width,
    )[0]


def local(
    tokens,
    lengths,
    gain_one,
    shift_one,
    w_qkv,
    b_qkv,
    w_dense,
    b_dense,
    gain_two,
    shift_two,
    w_up,
    b_up,
    w_down,
    b_down,
    cotangent,
):
    _, span, D = tokens.shape
    chips = lax.axis_size("z") * 2
    W = chips * 2
    G = chips // HEADS
    L = span * W
    R = w_qkv.shape[0]
    H2 = R // 2
    HK = HEAD_DIM // 2
    QW = 3 * HK
    FW = w_down.shape[0]
    FF = w_up.shape[1]
    z, y, k, d = (lax.axis_index(a) for a in ("z", "y", "core", "dp"))
    chip = z * 2 + y
    me = chip * 2 + k
    head = chip // G

    vectors = (gain_one, shift_one, gain_two, shift_two, b_qkv, b_dense, b_down, b_up)
    small = jnp.concatenate(vectors)
    small = jnp.pad(small, (0, TAIL * QW - small.shape[0])).reshape(1, TAIL, QW)
    u_rows = pick(w_up.reshape(2, H2, W, FW), d).transpose(1, 0, 2)
    u_got = lax.all_to_all(u_rows, WIDE, 0, 0, tiled=True)
    q_rows = pick(w_qkv.reshape(2, H2, 3, HEADS, 2, HK), d)
    q_rows = q_rows.transpose(2, 3, 0, 1, 4).reshape(HEADS, 1, 2, H2, QW)
    q_rows = jnp.broadcast_to(q_rows, (HEADS, G, 2, H2, QW)).reshape(W, H2, QW)
    q_sent = jnp.concatenate([q_rows, jnp.broadcast_to(small, (W, TAIL, QW))], axis=1)
    q_got = lax.all_to_all(q_sent, WIDE, 0, 0, tiled=True)

    def whole(got):
        return pair(d, got, swap(got, "dp"), axis=1).reshape(D, got.shape[-1])

    wu_own = whole(u_got)
    wu_other = swap(wu_own, "core")
    wq_own = whole(q_got[:, :H2])
    wq_other = swap(wq_own, "core")
    small_all = q_got[:, H2:].reshape(W, TAIL * QW)
    pieces = []
    start = 0
    for piece in vectors:
        pieces.append(small_all[:, start : start + piece.shape[0]].astype(f32))
        start += piece.shape[0]
    g1, s1, g2, s2, bq_all, bd_all, bo_all = (piece.reshape(-1) for piece in pieces[:-1])
    bu_all = pieces[-1]
    bu_own, bu_other = pick(bu_all, me), pick(bu_all, me + 1 - 2 * k)
    bq_head = pick(bq_all.reshape(3, HEADS, 2, HK), head, 1)
    bq_own, bq_other = (pick(bq_head, at, 1).reshape(QW) for at in (k, 1 - k))
    if G == 1:
        wd = jnp.concatenate([w_dense, swap(w_dense, "core")], axis=0)
    else:
        wd = pick(lax.all_gather(w_dense, WIDE).reshape(HEADS, 2, HK, D), head)
        wd = jnp.concatenate([pick(wd, k), pick(wd, 1 - k)], axis=0)
    w_down_other = swap(w_down, "core")
    wo = jnp.concatenate([w_down, w_down_other, wd], axis=0)

    def own_seq(array):
        return jnp.concatenate(
            [pick(array, k), swap(pick(array, 1 - k), "core")], axis=0
        )

    x_chip = own_seq(tokens)
    c_chip = own_seq(cotangent)
    length = pick(lengths, k)
    x_all = gather_rows(x_chip)
    c_all = gather_rows(c_chip)

    both = jnp.arange(2, dtype=jnp.int32)
    in_chip = ((both ^ k)[:, None] * span + jnp.arange(span, dtype=jnp.int32)).reshape(2 * span)
    place = (jnp.arange(chips, dtype=jnp.int32)[:, None] * (2 * span) + in_chip).reshape(L)
    place_chip = chip * (2 * span) + in_chip

    cosine, sine = rotary_tables(place)
    flat = jnp.zeros((L, HK - ROT), f32)
    nil = jnp.zeros((L, ROT // 2), f32)
    at_core = ((both ^ k) == 0)[None, :, None]

    def table(turned, otherwise):
        return jnp.where(at_core, turned[:, None, :], otherwise).reshape(L, 2 * HK)

    cos_t = table(jnp.concatenate([cosine, cosine, flat + 1.0], axis=1), 1.0)
    low_t = table(jnp.concatenate([sine, nil, flat], axis=1), 0.0)
    high_t = table(jnp.concatenate([nil, sine, flat], axis=1), 0.0)
    ok = (place < length).astype(f32).reshape(L, 1)
    row_place = place.reshape(L, 1)
    col_place = jnp.where(place < length, place, jnp.int32(2**30)).reshape(1, L)

    rows = 4 * span
    steps = L // rows
    norms = jnp.stack([g1, s1, g2, s2])
    h1, h2, act_own, act_other, slope_own, slope_other, queries, keys, values = call(
        front_kernel,
        "norm_up_qkv",
        steps,
        [
            (x_all, (rows, D)),
            (ok, (rows, 1)),
            (norms, None),
            (wu_own, None),
            (wu_other, None),
            (wq_own, None),
            (wq_other, None),
            (jnp.stack([bu_own, bu_other]), None),
            (jnp.stack([bq_own, bq_other]), None),
            (cos_t, (rows, 2 * HK)),
            (low_t, (rows, 2 * HK)),
            (high_t, (rows, 2 * HK)),
        ],
        [((L, D), bf16, (rows, D))] * 2
        + [((L, FW), bf16, (rows, FW))] * 2
        + [((L, FW), f32, (rows, FW))] * 2
        + [((L, HEAD_DIM), bf16, (rows, HEAD_DIM))] * 3,
        flops=2 * L * D * (2 * FW + 2 * QW),
    )
    score_scale = HEAD_DIM ** (-0.5)
    mine = (place // (L // G) == chip % G)[:, None]
    attended, lse = call(
        functools.partial(attend_kernel, score_scale),
        "attend",
        1,
        [(a, None) for a in (queries, keys, values, ok, row_place, col_place)],
        [((L, HEAD_DIM), bf16, None), ((L, 1), f32, None)],
        flops=4 * L * L * HEAD_DIM,
    )
    if G > 1:
        attended = jnp.where(mine, attended, jnp.zeros((), bf16))

    mixed_part, mixed_done = call(
        out_kernel,
        "dense_down",
        steps,
        [
            (act_own, (rows, FW)),
            (act_other, (rows, FW)),
            (attended, (rows, HEAD_DIM)),
            (w_down, None),
            (w_down_other, None),
            (wd, None),
        ],
        [((L, D), bf16, (rows, D)), ((8, 128), f32, None)],
        flops=2 * L * D * (2 * FW + HEAD_DIM),
    )
    mixed_sum = scatter_rows(mixed_part)

    gu_own, gu_other, ga, gb_u, gb_o = call(
        back_kernel,
        "back_dense_down",
        steps,
        [
            (c_all, (rows, D)),
            (ok, (rows, 1)),
            (slope_own, (rows, FW)),
            (slope_other, (rows, FW)),
            (w_down, None),
            (w_down_other, None),
            (wd, None),
        ],
        [
            ((L, FW), bf16, (rows, FW)),
            ((L, FW), bf16, (rows, FW)),
            ((L, HEAD_DIM), bf16, (rows, HEAD_DIM)),
            ((2, FW), f32, None),
            ((1, D), f32, None),
        ],
        order=(mixed_done,),
        flops=2 * L * D * (2 * FW + HEAD_DIM),
    )
    if G > 1:
        ga = jnp.where(mine, ga, jnp.zeros((), bf16))
    at_d = d.astype(jnp.int32).reshape(1)
    part = FW // 2 if FW % 256 == 0 else FW
    up_other = turned_product("grad_up_other", h2, gu_other)
    down_other = turned_product("grad_down_other", act_other, c_all, count=part, order=(up_other,))
    gb_o = jnp.concatenate(
        [lax.dynamic_slice_in_dim(gb_o[0], at * R, R) for at in (me, me + 1 - 2 * k)]
    )

    def over_cores(own, other):
        return own + swap(other, "core")

    bias = over_cores(
        jnp.concatenate([gb_u[0], gb_o[:R]]), jnp.concatenate([gb_u[1], gb_o[R:]])
    )
    gb_u, gb_o = bias[:FW], bias[FW:]

    up_mine, up_send = turned_product(
        "grad_up_own",
        h2,
        gu_own,
        got=swap(up_other, "core"),
        halves=(at_d, H2),
        order=(down_other, bias),
    )

    gj_own, gj_other, gb_j = call(
        functools.partial(attend_back_kernel, score_scale),
        "back_attend",
        1,
        [
            (a, None)
            for a in (queries, keys, values, ga, lse, row_place, col_place, cos_t, low_t, high_t)
        ],
        [((L, QW), bf16, None), ((L, QW), bf16, None), ((2, QW), f32, None)],
        scratch=[pltpu.VMEM((L, HEAD_DIM), f32)] * 2,
        order=(up_mine,),
        flops=10 * L * L * HEAD_DIM,
    )

    qkv_other = turned_product("grad_qkv_other", h1, gj_other)
    down_own = turned_product(
        "grad_down_own", act_own, c_all, got=swap(down_other, "core"), count=part,
        order=(qkv_other,),
    )
    down_dp = swap(down_own, "dp")
    gb_q = over_cores(gb_j[0], gb_j[1])
    qkv_mine, qkv_send = turned_product(
        "grad_qkv_own",
        h1,
        gj_own,
        got=swap(qkv_other, "core"),
        halves=(at_d, H2),
        order=(down_own, gb_q),
    )
    up_half = half_sum("half_up", up_mine, up_send, gb_u, (qkv_mine,))

    f_part, f_done = call(
        in_kernel,
        "back_up_qkv",
        steps,
        [
            (gj_own, (rows, QW)),
            (gj_other, (rows, QW)),
            (gu_own, (rows, FW)),
            (gu_other, (rows, FW)),
            (wq_own, None),
            (wq_other, None),
            (wu_own, None),
            (wu_other, None),
            (norms, None),
        ],
        [((L, D), bf16, (rows, D)), ((8, 128), f32, None)],
        order=(up_half,),
        flops=2 * L * D * (2 * FW + 2 * QW),
    )
    qkv_half = half_sum("half_qkv", qkv_mine, qkv_send, gb_q, (f_done,))
    f_sum = scatter_rows(gate(f_part, mixed_sum, qkv_half))
    up_got = lax.all_to_all(up_half, WIDE, 0, 0, tiled=True)
    last = (qkv_half,)
    if part < FW:
        rest_other = turned_product(
            "grad_down_other2", act_other, c_all, start=part, order=last
        )
        last = (rest_other,)
    dense_other = turned_product("grad_dense_other", attended, c_all, start=HK, order=last)
    dense_got = swap(dense_other, "core") if G == 1 else jnp.zeros_like(dense_other)
    downs = [(down_own, down_dp)]
    last = (dense_other,)
    if part < FW:
        rest_own = turned_product(
            "grad_down_own2", act_own, c_all, got=swap(rest_other, "core"), start=part,
            order=last,
        )
        downs.append((rest_own, swap(rest_own, "dp")))
        last = (rest_own,)
    dense_own = turned_product(
        "grad_dense_own", attended, c_all, got=dense_got, count=HK, order=last
    )
    ok_chip = (place_chip < length)[:, None]
    x_chip_f = x_chip.astype(f32)
    mixed_chip = jnp.where(ok_chip, x_chip_f + mixed_sum + (bd_all + bo_all), 0.0).astype(bf16)

    def own_positions(rows):
        return pair(k, rows[:span], swap(rows[span:], "core"))

    mixed = own_positions(mixed_chip)

    n_chip, r_chip = norm_stats(x_chip_f)
    grad_x = r_chip * (
        f_sum
        - jnp.mean(f_sum, axis=-1, keepdims=True)
        - n_chip * jnp.mean(f_sum * n_chip, axis=-1, keepdims=True)
    )
    go_chip = jnp.where(ok_chip, c_chip.astype(f32), 0.0)
    token_grad = own_positions((go_chip + grad_x).astype(bf16))

    gw_down = jnp.concatenate([own.astype(f32) + got.astype(f32) for own, got in downs], axis=0)
    if G > 1:
        dense = pair(k, dense_own, dense_other).reshape(1, HEAD_DIM, D).astype(f32)
        at_head = (jnp.arange(HEADS) == head)[:, None, None]
        dense = jnp.where(at_head, dense, 0.0).reshape(D, D)
        dense_own = lax.psum_scatter(dense, WIDE, scatter_dimension=0, tiled=True).astype(bf16)
    gw_dense = dense_own.astype(f32) + swap(dense_own, "dp").astype(f32)

    def norm_grads(product, shift_grad, gain, shift):
        return ((product - shift.astype(f32) * shift_grad) / gain.astype(f32), shift_grad)

    def tail_of(own, other):
        return own[:, H2].astype(f32) + other[:, H2].astype(f32)

    qkv_got = lax.all_to_all(gate(qkv_half, up_got, dense_own), WIDE, 0, 0, tiled=True)
    up_dp = swap(up_got, "dp")
    qkv_dp = swap(qkv_got, "dp")
    gw_up, up_sum, up_shift = weight_rows("rows_up", at_d, up_got, up_dp, w_up, FW)
    gg2, gs2 = norm_grads(up_sum, up_shift, gain_two, shift_two)
    gb_up = pick(tail_of(up_got, up_dp), me)
    gb_out = gb_o + swap(gb_o, "dp")
    gb_q_all = tail_of(qkv_got, qkv_dp)
    gb_q_all = gb_q_all.reshape(HEADS, G, 2, 3, HK).sum(1).transpose(2, 0, 1, 3).reshape(3 * D)
    if G == 1:
        gw_q, q_sum, q_shift = weight_rows(
            "rows_qkv", at_d, qkv_got, qkv_dp, w_qkv, HK, order=(mixed, token_grad)
        )
    else:
        gw_q = pair(d, qkv_got[:, :H2], qkv_dp[:, :H2]).astype(f32)
        gw_q = gw_q.reshape(2, HEADS, G, 2, H2, 3, HK).sum(2)
        gw_q = gw_q.transpose(0, 3, 4, 1, 2, 5).reshape(R, 3 * D)
        wf = w_qkv.astype(f32)
        q_sum, q_shift = jnp.sum(wf * gw_q, axis=1), jnp.sum(wf * gb_q_all[None, :], axis=1)
    gg1, gs1 = norm_grads(q_sum, q_shift, gain_one, shift_one)
    gb_qkv = lax.dynamic_slice_in_dim(gb_q_all, me * 3 * R, 3 * R)
    return (
        mixed,
        token_grad,
        gg1,
        gs1,
        gw_q,
        gb_qkv,
        gw_dense,
        gb_out,
        gg2,
        gs2,
        gw_up,
        gb_up,
        gw_down,
        gb_out,
    )


def solution(mesh):
    dp, wide = mesh.shape["dp"], mesh.shape["wide"]
    split = Mesh(mesh.devices.reshape(dp, wide // 4, 2, 2), ("dp",) + WIDE)
    rows = P("dp", WIDE, None)
    mat, vec = P(WIDE, None), P(WIDE)
    in_specs = (rows, P("dp"), vec, vec, mat, vec, mat, vec, vec, vec, mat, vec, mat, vec, rows)
    out_specs = (rows, rows, vec, vec, mat, vec, mat, vec, vec, vec, mat, vec, mat, vec)
    return jax.shard_map(local, mesh=split, in_specs=in_specs, out_specs=out_specs, check_vma=False)
```

```python
import functools
import math

import jax
import jax.numpy as jnp
from jax import lax
from jax.experimental import pallas as pl
from jax.experimental.pallas import tpu as pltpu
from jax.sharding import Mesh
from jax.sharding import PartitionSpec as P

HEADS = 8
HEAD_DIM = 256
ROT = 64

EPS = 1e-05
MASKED = -1e30
ROT_BASE = 10000.0
ROOT_HALF = 0.7071067811865476
INV_ROOT_TAU = 0.3989422804014327

WIDE = ("z", "y", "core")
CHIPS = ("z", "y")
TAIL = 8
BLOCK = 256
VMEM_BYTES = 58 * 1024 * 1024
f32 = jnp.float32
bf16 = jnp.bfloat16


def rotary_tables(places):
    halves = ROT // 2
    inverse = ROT_BASE ** (-2.0 * jnp.arange(halves, dtype=f32) / ROT)
    angles = places.astype(f32)[:, None] * inverse[None, :]
    return (jnp.cos(angles), jnp.sin(angles))


def norm_stats(values):
    average = jnp.mean(values, axis=-1, keepdims=True)
    centered = values - average
    variance = jnp.mean(centered * centered, axis=-1, keepdims=True)
    scale = lax.rsqrt(variance + EPS)
    return (centered * scale, scale)


def swap(part, axis):
    return lax.ppermute(part, axis, [(0, 1), (1, 0)])


def pair(index, own, other, axis=0):
    return jnp.where(
        index == 0, jnp.stack([own, other], axis=axis), jnp.stack([other, own], axis=axis)
    )


def dot(a, b, dims, out=f32):
    return lax.dot_general(a, b, (dims, ((), ())), preferred_element_type=f32).astype(out)


NN = ((1,), (0,))
NT = ((1,), (1,))
TN = ((0,), (0,))


def pick(array, index, axis=0):
    return lax.dynamic_index_in_dim(array, index, axis, keepdims=False)


def gather_rows(own):
    return lax.all_gather(own, CHIPS, axis=0, tiled=True)


def rows_kernel(d, own, other, w, out, sums):
    @pl.when(pl.program_id(0) == 0)
    def _():
        sums[...] = jnp.zeros_like(sums)

    half = out.shape[0] // 2
    width = own.shape[2]
    for j in range(own.shape[0]):
        cols = slice(j * width, (j + 1) * width)
        mine, got = own[j].astype(f32), other[j].astype(f32)
        bias = mine[half : half + 1] + got[half : half + 1]
        for at in range(2):
            rows = slice(at * half, (at + 1) * half)
            grad = jnp.where(d[0] == at, mine[:half], got[:half])
            out[rows, cols] = grad
            weight = w[rows, cols].astype(f32)
            sums[rows, 0:1] += jnp.sum(weight * grad, axis=1, keepdims=True)
            sums[rows, 1:2] += jnp.sum(weight * bias, axis=1, keepdims=True)


def weight_rows(name, d, own, other, w, width, order=()):
    devices, height, columns = own.shape
    rows = w.shape[0]
    group = math.gcd(2048 // width, devices)
    blocks = devices // group
    shape = (group, height, width)
    at = lambda i: (lax.rem(i, blocks), 0, lax.div(i, blocks))
    grad, sums = call(
        rows_kernel,
        name,
        blocks * (columns // width),
        [
            (d, "scalars"),
            (own, shape, at),
            (other, shape, at),
            (w, (rows, group * width), lambda i: (0, i)),
        ],
        [((rows, w.shape[1]), f32, (rows, group * width), lambda i: (0, i)), ((rows, 2), f32, None)],
        order=order,
    )
    return (grad, sums[:, 0], sums[:, 1])


def half_kernel(mine, got, row, out):
    total = (mine[...].astype(f32) + got[...].astype(f32)).astype(bf16)
    tail = (out.shape[0], out.shape[1] - total.shape[1], out.shape[2])
    row = jnp.broadcast_to(row[...][None], tail).astype(bf16)
    out[...] = jnp.concatenate([total, row], axis=1)


def half_sum(name, mine, send, row, order):
    devices, rows, width = mine.shape
    return call(
        half_kernel,
        name,
        1,
        [(mine, None), (swap(send, "dp"), None), (row.reshape(1, width), None)],
        [((devices, rows + TAIL, width), bf16, None)],
        order=order,
    )[0]


def gate(value, *others):
    spec = pl.BlockSpec(memory_space=pl.ANY)
    return pl.pallas_call(
        lambda *refs: None,
        in_specs=[spec] * (1 + len(others)),
        out_specs=spec,
        out_shape=jax.ShapeDtypeStruct(value.shape, value.dtype),
        input_output_aliases={0: 0},
        name="gate",
    )(value, *others)


def scatter_rows(part):
    return lax.psum_scatter(part, CHIPS, scatter_dimension=0, tiled=True)


def call(kernel, name, grid, ins, outs, scratch=(), order=(), flops=0):
    def whole(shape):
        return pl.BlockSpec(shape, lambda i: (0,) * len(shape))

    def blocked(shape, block, at=None):
        if block == "scalars":
            return pl.BlockSpec(memory_space=pltpu.SMEM)
        if block is None:
            return whole(shape)
        return pl.BlockSpec(block, at or (lambda i: (i,) + (0,) * (len(block) - 1)))

    def run(*refs):
        kernel(*refs[: len(ins)], *refs[len(ins) + len(order) :])

    arrays = [entry[0] for entry in ins]
    moved = sum(a.size * a.dtype.itemsize for a in arrays)
    moved += sum(functools.reduce(lambda p, n: p * n, o[0], 1) * o[1].dtype.itemsize for o in outs)
    return pl.pallas_call(
        run,
        grid=(grid,),
        in_specs=[blocked(entry[0].shape, *entry[1:]) for entry in ins]
        + [pl.BlockSpec(memory_space=pl.ANY)] * len(order),
        out_specs=[blocked(o[0], *o[2:]) for o in outs],
        out_shape=[jax.ShapeDtypeStruct(o[0], o[1]) for o in outs],
        scratch_shapes=list(scratch),
        compiler_params=pltpu.CompilerParams(
            vmem_limit_bytes=VMEM_BYTES, dimension_semantics=("arbitrary",)
        ),
        cost_estimate=pl.CostEstimate(flops=flops, bytes_accessed=moved, transcendentals=0),
        name=name,
    )(*arrays, *order)


def turn(half, c_ref, down_ref, up_ref, way):
    width, step = half.shape[-1], ROT // 2
    ahead = pltpu.roll(half, width - step, 1) * down_ref
    behind = pltpu.roll(half, step, 1) * up_ref
    return half * c_ref + way * (behind - ahead)


def part_rows(at, total, own, other):
    rows = own.shape[0]
    first = at[0] == 0
    own[...] = jnp.where(first, total[:rows], total[rows:])
    other[...] = jnp.where(first, total[rows:], total[:rows])


def front_kernel(x, ok, norms, wuo, wux, wqo, wqx, bu, bq, cos, low, high, h1, h2, acto, actx, slo, slx, q, k, v):
    n, _ = norm_stats(x[...].astype(f32))
    first = (n * norms[0:1, :] + norms[1:2, :]).astype(bf16)
    second = (n * norms[2:3, :] + norms[3:4, :]).astype(bf16)
    h1[...] = first
    h2[...] = second
    for at, (w, act, slope) in enumerate(((wuo, acto, slo), (wux, actx, slx))):
        upper = dot(second, w[...], NN) + bu[at : at + 1, :]
        cdf = 0.5 * (1.0 + lax.erf(upper * ROOT_HALF))
        act[...] = (upper * cdf * ok[...]).astype(bf16)
        slope[...] = cdf + upper * jnp.exp(-0.5 * upper * upper) * INV_ROOT_TAU
    for at, w in enumerate((wqo, wqx)):
        joined = dot(first, w[...], NN) + bq[at : at + 1, :]
        wide = joined.shape[1] // 3
        cols = slice(at * wide, (at + 1) * wide)
        tables = (cos[:, cols], low[:, cols], high[:, cols])
        q[:, cols] = turn(joined[:, :wide], *tables, 1.0).astype(bf16)
        k[:, cols] = turn(joined[:, wide : 2 * wide], *tables, 1.0).astype(bf16)
        v[:, cols] = joined[:, 2 * wide :].astype(bf16)


def weights_of(q, k, row_place, col_place, scale):
    scores = dot(q, k, NT) * scale
    return jnp.where(col_place <= row_place, scores, MASKED)


def attend_kernel(scale, q, k, v, ok, row_place, col_place, att, lse):
    rows = q.shape[0]
    step = min(BLOCK, rows)
    for start in range(0, rows, step):
        mine, seen = slice(start, start + step), slice(0, start + step)
        scores = weights_of(q[mine, :], k[seen, :], row_place[mine, :], col_place[:, seen], scale)
        top = jnp.max(scores, axis=1, keepdims=True)
        raised = jnp.exp(scores - top)
        total = jnp.sum(raised, axis=1, keepdims=True)
        weights = (raised * (1.0 / total)).astype(bf16)
        att[mine, :] = (dot(weights, v[seen, :], NN) * ok[mine, :]).astype(bf16)
        lse[mine, :] = top + jnp.log(total)


def attend_back_kernel(scale, q, k, v, ga, lse, row_place, col_place, cos, low, high, gjo, gjx, sums, gk, gv):
    rows = q.shape[0]
    step = min(BLOCK, rows)
    gk[...] = jnp.zeros_like(gk)
    gv[...] = jnp.zeros_like(gv)
    wide = q.shape[1] // 2
    for start in range(0, rows, step):
        mine, seen = slice(start, start + step), slice(0, start + step)
        scores = weights_of(q[mine, :], k[seen, :], row_place[mine, :], col_place[:, seen], scale)
        soft = jnp.exp(scores - lse[mine, :])
        g_soft = dot(ga[mine, :], v[seen, :], NT)
        product = soft * g_soft
        delta = jnp.sum(product, axis=1, keepdims=True)
        g_scores = (product - soft * delta).astype(bf16)
        gk[seen, :] += dot(g_scores, q[mine, :], TN)
        gv[seen, :] += dot(soft.astype(bf16), ga[mine, :], TN)
        g_q = dot(g_scores, k[seen, :], NN) * scale
        for at, out in enumerate((gjo, gjx)):
            cols = slice(at * wide, (at + 1) * wide)
            tables = (cos[mine, cols], low[mine, cols], high[mine, cols])
            out[mine, :wide] = turn(g_q[:, cols], *tables, -1.0).astype(bf16)
    for start in range(0, rows, step):
        mine = slice(start, start + step)
        for at, out in enumerate((gjo, gjx)):
            cols = slice(at * wide, (at + 1) * wide)
            tables = (cos[mine, cols], low[mine, cols], high[mine, cols])
            out[mine, wide : 2 * wide] = turn(gk[mine, cols] * scale, *tables, -1.0).astype(bf16)
            out[mine, 2 * wide :] = gv[mine, cols].astype(bf16)
    for at, out in enumerate((gjo, gjx)):
        sums[at : at + 1, :] = jnp.sum(out[...].astype(f32), axis=0, keepdims=True)


def out_kernel(acto, actx, att, wo, wx, wd, out, done):
    total = dot(acto[...], wo[...], NN) + dot(actx[...], wx[...], NN) + dot(att[...], wd[...], NN)
    out[...] = total.astype(bf16)
    done[...] = jnp.zeros_like(done)


def back_kernel(c, ok, slo, slx, wo, wx, wd, guo, gux, ga, sums, sum_go):
    @pl.when(pl.program_id(0) == 0)
    def _():
        sums[...] = jnp.zeros_like(sums)
        sum_go[...] = jnp.zeros_like(sum_go)

    grad = jnp.where(ok[...] > 0, c[...], jnp.zeros((), bf16))
    for at, (w, slope, gu) in enumerate(((wo, slo, guo), (wx, slx, gux))):
        low = (dot(grad, w[...], NT) * slope[...]).astype(bf16)
        gu[...] = low
        sums[at : at + 1, :] += jnp.sum(low.astype(f32), axis=0, keepdims=True)
    ga[...] = dot(grad, wd[...], NT, bf16)
    sum_go[...] += jnp.sum(grad.astype(f32), axis=0, keepdims=True)


def in_kernel(gjo, gjx, guo, gux, wqo, wqx, wuo, wux, norms, out, done):
    one = dot(gjo[...], wqo[...], NT) + dot(gjx[...], wqx[...], NT)
    two = dot(guo[...], wuo[...], NT) + dot(gux[...], wux[...], NT)
    out[...] = (one * norms[0:1, :] + two * norms[2:3, :]).astype(bf16)
    done[...] = jnp.zeros_like(done)


def turned_kernel(left, right, *rest):
    total = dot(left[...], right[...], TN)
    if len(rest) == 2:
        total = total + rest[0][...].astype(f32)
    rest[-1][...] = total.astype(bf16)


def turned_half_kernel(d, left, right, got, mine, other):
    total = (dot(left[...], right[...], TN) + got[...].astype(f32)).astype(bf16)
    rows = mine.shape[1]
    for i in range(mine.shape[0]):
        at = slice(2 * i * rows, 2 * (i + 1) * rows)
        part_rows(d, total[at], mine.at[i], other.at[i])


def turned_product(name, left, right, got=None, start=0, count=None, halves=None, order=()):
    depth = left.shape[0]
    count = count or left.shape[1] - start
    width = right.shape[1]
    block = math.gcd(BLOCK, count)
    first = start // block
    ins = [(left, (depth, block), lambda i: (0, first + i)), (right, None)]
    if got is not None:
        ins.append((got, (block, width)))
    if halves:
        place, rows = halves
        blocks = (block // (2 * rows), rows, width)
        return call(
            turned_half_kernel,
            name,
            count // block,
            [(place, "scalars")] + ins,
            [((count // (2 * rows), rows, width), bf16, blocks)] * 2,
            order=order,
            flops=2 * depth * count * width,
        )
    return call(
        turned_kernel,
        name,
        count // block,
        ins,
        [((count, width), bf16, (block, width))],
        order=order,
        flops=2 * depth * count * width,
    )[0]


def local(
    tokens,
    lengths,
    gain_one,
    shift_one,
    w_qkv,
    b_qkv,
    w_dense,
    b_dense,
    gain_two,
    shift_two,
    w_up,
    b_up,
    w_down,
    b_down,
    cotangent,
):
    _, span, D = tokens.shape
    chips = lax.axis_size("z") * 2
    W = chips * 2
    G = chips // HEADS
    L = span * W
    R = w_qkv.shape[0]
    H2 = R // 2
    HK = HEAD_DIM // 2
    QW = 3 * HK
    FW = w_down.shape[0]
    FF = w_up.shape[1]
    z, y, k, d = (lax.axis_index(a) for a in ("z", "y", "core", "dp"))
    chip = z * 2 + y
    me = chip * 2 + k
    head = chip // G

    vectors = (gain_one, shift_one, gain_two, shift_two, b_qkv, b_dense, b_down, b_up)
    small = jnp.concatenate(vectors)
    small = jnp.pad(small, (0, TAIL * QW - small.shape[0])).reshape(1, TAIL, QW)
    u_rows = pick(w_up.reshape(2, H2, W, FW), d).transpose(1, 0, 2)
    u_got = lax.all_to_all(u_rows, WIDE, 0, 0, tiled=True)
    q_rows = pick(w_qkv.reshape(2, H2, 3, HEADS, 2, HK), d)
    q_rows = q_rows.transpose(2, 3, 0, 1, 4).reshape(HEADS, 1, 2, H2, QW)
    q_rows = jnp.broadcast_to(q_rows, (HEADS, G, 2, H2, QW)).reshape(W, H2, QW)
    q_sent = jnp.concatenate([q_rows, jnp.broadcast_to(small, (W, TAIL, QW))], axis=1)
    q_got = lax.all_to_all(q_sent, WIDE, 0, 0, tiled=True)

    def whole(got):
        return pair(d, got, swap(got, "dp"), axis=1).reshape(D, got.shape[-1])

    wu_own = whole(u_got)
    wu_other = swap(wu_own, "core")
    wq_own = whole(q_got[:, :H2])
    wq_other = swap(wq_own, "core")
    small_all = q_got[:, H2:].reshape(W, TAIL * QW)
    pieces = []
    start = 0
    for piece in vectors:
        pieces.append(small_all[:, start : start + piece.shape[0]].astype(f32))
        start += piece.shape[0]
    g1, s1, g2, s2, bq_all, bd_all, bo_all = (piece.reshape(-1) for piece in pieces[:-1])
    bu_all = pieces[-1]
    bu_own, bu_other = pick(bu_all, me), pick(bu_all, me + 1 - 2 * k)
    bq_head = pick(bq_all.reshape(3, HEADS, 2, HK), head, 1)
    bq_own, bq_other = (pick(bq_head, at, 1).reshape(QW) for at in (k, 1 - k))
    if G == 1:
        wd = jnp.concatenate([w_dense, swap(w_dense, "core")], axis=0)
    else:
        wd = pick(lax.all_gather(w_dense, WIDE).reshape(HEADS, 2, HK, D), head)
        wd = jnp.concatenate([pick(wd, k), pick(wd, 1 - k)], axis=0)
    w_down_other = swap(w_down, "core")
    wo = jnp.concatenate([w_down, w_down_other, wd], axis=0)

    def own_seq(array):
        return jnp.concatenate(
            [pick(array, k), swap(pick(array, 1 - k), "core")], axis=0
        )

    x_chip = own_seq(tokens)
    c_chip = own_seq(cotangent)
    length = pick(lengths, k)
    x_all = gather_rows(x_chip)
    c_all = gather_rows(c_chip)

    both = jnp.arange(2, dtype=jnp.int32)
    in_chip = ((both ^ k)[:, None] * span + jnp.arange(span, dtype=jnp.int32)).reshape(2 * span)
    place = (jnp.arange(chips, dtype=jnp.int32)[:, None] * (2 * span) + in_chip).reshape(L)
    place_chip = chip * (2 * span) + in_chip

    cosine, sine = rotary_tables(place)
    flat = jnp.zeros((L, HK - ROT), f32)
    nil = jnp.zeros((L, ROT // 2), f32)
    at_core = ((both ^ k) == 0)[None, :, None]

    def table(turned, otherwise):
        return jnp.where(at_core, turned[:, None, :], otherwise).reshape(L, 2 * HK)

    cos_t = table(jnp.concatenate([cosine, cosine, flat + 1.0], axis=1), 1.0)
    low_t = table(jnp.concatenate([sine, nil, flat], axis=1), 0.0)
    high_t = table(jnp.concatenate([nil, sine, flat], axis=1), 0.0)
    ok = (place < length).astype(f32).reshape(L, 1)
    row_place = place.reshape(L, 1)
    col_place = jnp.where(place < length, place, jnp.int32(2**30)).reshape(1, L)

    rows = 4 * span
    steps = L // rows
    norms = jnp.stack([g1, s1, g2, s2])
    h1, h2, act_own, act_other, slope_own, slope_other, queries, keys, values = call(
        front_kernel,
        "norm_up_qkv",
        steps,
        [
            (x_all, (rows, D)),
            (ok, (rows, 1)),
            (norms, None),
            (wu_own, None),
            (wu_other, None),
            (wq_own, None),
            (wq_other, None),
            (jnp.stack([bu_own, bu_other]), None),
            (jnp.stack([bq_own, bq_other]), None),
            (cos_t, (rows, 2 * HK)),
            (low_t, (rows, 2 * HK)),
            (high_t, (rows, 2 * HK)),
        ],
        [((L, D), bf16, (rows, D))] * 2
        + [((L, FW), bf16, (rows, FW))] * 2
        + [((L, FW), f32, (rows, FW))] * 2
        + [((L, HEAD_DIM), bf16, (rows, HEAD_DIM))] * 3,
        flops=2 * L * D * (2 * FW + 2 * QW),
    )
    score_scale = HEAD_DIM ** (-0.5)
    mine = (place // (L // G) == chip % G)[:, None]
    attended, lse = call(
        functools.partial(attend_kernel, score_scale),
        "attend",
        1,
        [(a, None) for a in (queries, keys, values, ok, row_place, col_place)],
        [((L, HEAD_DIM), bf16, None), ((L, 1), f32, None)],
        flops=4 * L * L * HEAD_DIM,
    )
    if G > 1:
        attended = jnp.where(mine, attended, jnp.zeros((), bf16))

    mixed_part, mixed_done = call(
        out_kernel,
        "dense_down",
        steps,
        [
            (act_own, (rows, FW)),
            (act_other, (rows, FW)),
            (attended, (rows, HEAD_DIM)),
            (w_down, None),
            (w_down_other, None),
            (wd, None),
        ],
        [((L, D), bf16, (rows, D)), ((8, 128), f32, None)],
        flops=2 * L * D * (2 * FW + HEAD_DIM),
    )
    mixed_sum = scatter_rows(mixed_part)

    gu_own, gu_other, ga, gb_u, gb_o = call(
        back_kernel,
        "back_dense_down",
        steps,
        [
            (c_all, (rows, D)),
            (ok, (rows, 1)),
            (slope_own, (rows, FW)),
            (slope_other, (rows, FW)),
            (w_down, None),
            (w_down_other, None),
            (wd, None),
        ],
        [
            ((L, FW), bf16, (rows, FW)),
            ((L, FW), bf16, (rows, FW)),
            ((L, HEAD_DIM), bf16, (rows, HEAD_DIM)),
            ((2, FW), f32, None),
            ((1, D), f32, None),
        ],
        order=(mixed_done,),
        flops=2 * L * D * (2 * FW + HEAD_DIM),
    )
    if G > 1:
        ga = jnp.where(mine, ga, jnp.zeros((), bf16))
    at_d = d.astype(jnp.int32).reshape(1)
    part = 128 if FW % 128 == 0 else FW
    up_other = turned_product("grad_up_other", h2, gu_other)
    gb_o = jnp.concatenate(
        [lax.dynamic_slice_in_dim(gb_o[0], at * R, R) for at in (me, me + 1 - 2 * k)]
    )

    def over_cores(own, other):
        return own + swap(other, "core")

    bias = over_cores(
        jnp.concatenate([gb_u[0], gb_o[:R]]), jnp.concatenate([gb_u[1], gb_o[R:]])
    )
    gb_u, gb_o = bias[:FW], bias[FW:]

    gj_own, gj_other, gb_j = call(
        functools.partial(attend_back_kernel, score_scale),
        "back_attend",
        1,
        [
            (a, None)
            for a in (queries, keys, values, ga, lse, row_place, col_place, cos_t, low_t, high_t)
        ],
        [((L, QW), bf16, None), ((L, QW), bf16, None), ((2, QW), f32, None)],
        scratch=[pltpu.VMEM((L, HEAD_DIM), f32)] * 2,
        order=(up_other,),
        flops=10 * L * L * HEAD_DIM,
    )

    up_mine, up_send = turned_product(
        "grad_up_own",
        h2,
        gu_own,
        got=swap(up_other, "core"),
        halves=(at_d, H2),
        order=(gj_own, bias),
    )
    qkv_other = turned_product("grad_qkv_other", h1, gj_other, order=(up_mine,))
    down_other = turned_product("grad_down_other", act_other, c_all, count=part, order=(qkv_other,))
    down_own = turned_product(
        "grad_down_own", act_own, c_all, got=swap(down_other, "core"), count=part,
        order=(down_other,),
    )
    down_dp = swap(down_own, "dp")
    last = (down_own,)
    if part < FW:
        rest_other = turned_product(
            "grad_down_other2", act_other, c_all, start=part, order=last
        )
        last = (rest_other,)
    up_half = half_sum("half_up", up_mine, up_send, gb_u, last)
    up_got = lax.all_to_all(up_half, WIDE, 0, 0, tiled=True)
    gb_q = over_cores(gb_j[0], gb_j[1])
    qkv_mine, qkv_send = turned_product(
        "grad_qkv_own",
        h1,
        gj_own,
        got=swap(qkv_other, "core"),
        halves=(at_d, H2),
        order=(up_half, gb_q),
    )

    f_part, f_done = call(
        in_kernel,
        "back_up_qkv",
        steps,
        [
            (gj_own, (rows, QW)),
            (gj_other, (rows, QW)),
            (gu_own, (rows, FW)),
            (gu_other, (rows, FW)),
            (wq_own, None),
            (wq_other, None),
            (wu_own, None),
            (wu_other, None),
            (norms, None),
        ],
        [((L, D), bf16, (rows, D)), ((8, 128), f32, None)],
        order=(qkv_mine, down_dp),
        flops=2 * L * D * (2 * FW + 2 * QW),
    )
    qkv_half = half_sum("half_qkv", qkv_mine, qkv_send, gb_q, (f_done,))
    f_sum = scatter_rows(gate(f_part, mixed_sum, qkv_half, up_got)).astype(f32)
    last = (qkv_half,)
    dense_other = turned_product("grad_dense_other", attended, c_all, start=HK, order=last)
    dense_got = swap(dense_other, "core") if G == 1 else jnp.zeros_like(dense_other)
    downs = [(down_own, down_dp)]
    last = (dense_other,)
    if part < FW:
        rest_own = turned_product(
            "grad_down_own2", act_own, c_all, got=swap(rest_other, "core"), start=part,
            order=last,
        )
        downs.append((rest_own, swap(rest_own, "dp")))
        last = (rest_own,)
    dense_own = turned_product(
        "grad_dense_own", attended, c_all, got=dense_got, count=HK, order=last
    )
    ok_chip = (place_chip < length)[:, None]
    x_chip_f = x_chip.astype(f32)
    mixed_chip = jnp.where(ok_chip, x_chip_f + mixed_sum.astype(f32) + (bd_all + bo_all), 0.0).astype(bf16)

    def own_positions(rows):
        return pair(k, rows[:span], swap(rows[span:], "core"))

    mixed = own_positions(mixed_chip)

    n_chip, r_chip = norm_stats(x_chip_f)
    grad_x = r_chip * (
        f_sum
        - jnp.mean(f_sum, axis=-1, keepdims=True)
        - n_chip * jnp.mean(f_sum * n_chip, axis=-1, keepdims=True)
    )
    go_chip = jnp.where(ok_chip, c_chip.astype(f32), 0.0)
    token_grad = own_positions((go_chip + grad_x).astype(bf16))

    if G > 1:
        dense = pair(k, dense_own, dense_other).reshape(1, HEAD_DIM, D).astype(f32)
        at_head = (jnp.arange(HEADS) == head)[:, None, None]
        dense = jnp.where(at_head, dense, 0.0).reshape(D, D)
        dense_own = lax.psum_scatter(dense, WIDE, scatter_dimension=0, tiled=True).astype(bf16)
    gw_dense = dense_own.astype(f32) + swap(dense_own, "dp").astype(f32)

    def norm_grads(product, shift_grad, gain, shift):
        return ((product - shift.astype(f32) * shift_grad) / gain.astype(f32), shift_grad)

    def tail_of(own, other):
        return own[:, H2].astype(f32) + other[:, H2].astype(f32)

    qkv_got = lax.all_to_all(gate(qkv_half, up_got), WIDE, 0, 0, tiled=True)
    up_dp = swap(up_got, "dp")
    qkv_dp = swap(qkv_got, "dp")
    gw_up, up_sum, up_shift = weight_rows("rows_up", at_d, up_got, up_dp, w_up, FW, order=(qkv_got,))
    gg2, gs2 = norm_grads(up_sum, up_shift, gain_two, shift_two)
    gb_up = pick(tail_of(up_got, up_dp), me)
    gw_down = jnp.concatenate([own.astype(f32) + gate(got, gw_up).astype(f32) for own, got in downs], axis=0)
    gb_out = gb_o + gate(swap(gate(gb_o, qkv_got), "dp"), qkv_dp)
    gb_q_all = tail_of(qkv_got, qkv_dp)
    gb_q_all = gb_q_all.reshape(HEADS, G, 2, 3, HK).sum(1).transpose(2, 0, 1, 3).reshape(3 * D)
    if G == 1:
        gw_q, q_sum, q_shift = weight_rows("rows_qkv", at_d, qkv_got, qkv_dp, w_qkv, HK)
    else:
        gw_q = pair(d, qkv_got[:, :H2], qkv_dp[:, :H2]).astype(f32)
        gw_q = gw_q.reshape(2, HEADS, G, 2, H2, 3, HK).sum(2)
        gw_q = gw_q.transpose(0, 3, 4, 1, 2, 5).reshape(R, 3 * D)
        wf = w_qkv.astype(f32)
        q_sum, q_shift = jnp.sum(wf * gw_q, axis=1), jnp.sum(wf * gb_q_all[None, :], axis=1)
    gg1, gs1 = norm_grads(q_sum, q_shift, gain_one, shift_one)
    gb_qkv = lax.dynamic_slice_in_dim(gb_q_all, me * 3 * R, 3 * R)
    return (
        mixed,
        token_grad,
        gg1,
        gs1,
        gw_q,
        gb_qkv,
        gw_dense,
        gb_out,
        gg2,
        gs2,
        gw_up,
        gb_up,
        gw_down,
        gb_out,
    )


def solution(mesh):
    dp, wide = mesh.shape["dp"], mesh.shape["wide"]
    split = Mesh(mesh.devices.reshape(dp, wide // 4, 2, 2), ("dp",) + WIDE)
    rows = P("dp", WIDE, None)
    mat, vec = P(WIDE, None), P(WIDE)
    in_specs = (rows, P("dp"), vec, vec, mat, vec, mat, vec, vec, vec, mat, vec, mat, vec, rows)
    out_specs = (rows, rows, vec, vec, mat, vec, mat, vec, vec, vec, mat, vec, mat, vec)
    return jax.shard_map(local, mesh=split, in_specs=in_specs, out_specs=out_specs, check_vma=False)
```
